32 devices in a mesh: dp: 8 (over z, x), tensor: 4 (over y, core).
Axes of the slice: x: 2, y: 2, z: 4, core: 2. Of those that a mesh axis runs over, the one named last changes fastest.
Arguments:
- pre_act: bfloat16 [1024, 12288], P('dp', 'tensor'), may hold values from -6 to 6
- out_grad: bfloat16 [1024, 3072], P(('dp', 'tensor')), may hold values from -8 to 8
- w_up: bfloat16 [3072, 12288], P(None, 'tensor'), may hold values from -0.0546875 to 0.0546875
- w_down: bfloat16 [12288, 3072], P('tensor'), may hold values from -0.109375 to 0.109375
Outputs:
- in_grad: bfloat16 [1024, 3072], P(('dp', 'tensor'))
- down_grad_t: float32 [3072, 12288], P('dp', 'tensor')
The draws below stay inside these ranges and needn't reach their ends.
All inputs are finite; a program needn't handle non-finite values.
Results may differ from the reference program's by a relative error of at most 0.0049.
Values may be sent and summed in bfloat16 or wider, within the bound.
No kernel may reach another device: no remote copies, remote signals or barrier semaphores. Data moves between devices by JAX's collectives and lax.ppermute only.
A program may use at most 128 MiB of HBM per device.

```python
import math
import jax
import jax.numpy as jnp

D = 3072
FF = 12288
TOKENS = 1024


def strengthened(result, stream_key, source, target, shards_of, factor):
    def block_of(position):
        return (jnp.arange(result.shape[position]) // (result.shape[position] // shards_of)).reshape((-1,) + (1,) * (result.ndim - 1 - position))

    one_side = jax.random.permutation(stream_key, shards_of)[block_of(target)]
    other_side = (block_of(target) + shards_of // 2) % shards_of
    return jnp.where((block_of(source) == one_side) | (block_of(source) == other_side), factor * result, result)


def level_of(stream_key, extent, shards, smallest, high):
    loudness = 1.0
    for axis_at, blocks in shards:
        draws = jax.random.uniform(jax.random.fold_in(jax.random.fold_in(stream_key, 6), axis_at), (blocks,), jnp.float32, smallest / len(shards), high / len(shards))
        loudness = loudness * jnp.repeat(jnp.exp(draws), extent[axis_at] // blocks).reshape((-1,) + (1,) * (len(extent) - 1 - axis_at))
    return loudness


def bell_draw(stream_key, extent, width, most, cuts=(), kind=jnp.bfloat16):
    entries = width * jax.random.normal(stream_key, extent, jnp.float32)
    if cuts:
        entries = entries * level_of(stream_key, extent, cuts, -0.22, 0.18)
    return jnp.clip(entries, -most, most).astype(kind)


def gaussian_with(key, shape, scale, bound, split, heavy, held_as=jnp.bfloat16):
    entries = scale * jax.random.normal(key, shape, jnp.float32)
    if split:
        entries = entries * level_of(key, shape, split, -0.22, 0.18)
    return jnp.clip(strengthened(entries, jax.random.fold_in(key, 3), *heavy), -bound, bound).astype(held_as)


def setup_inputs(seed: int = 0) -> dict:
    key_of = jax.random.split(jax.random.key(seed), 5)
    pre_act = bell_draw(key_of[0], (TOKENS, FF), 1.0, 6.0, ((0, 8), (1, 4)))
    out_grad = gaussian_with(key_of[1], (TOKENS, D), 1.0, 8.0, ((0, 32),), (0, 1, 32, 2.75))
    w_up = bell_draw(key_of[2], (D, FF), FF ** -0.5, 0.0546875, ((1, 4),))
    w_down = bell_draw(key_of[3], (FF, D), D ** -0.5, 0.109375, ((0, 4),))
    return {"pre_act": pre_act, "out_grad": out_grad, "w_up": w_up, "w_down": w_down}


def gelu_parts(pre_float):
    normal_cdf = 0.5 * (1.0 + jax.scipy.special.erf(pre_float / math.sqrt(2.0)))
    density = jnp.exp(-0.5 * pre_float * pre_float) / math.sqrt(2.0 * math.pi)
    return (pre_float * normal_cdf, normal_cdf + pre_float * density)

def reference(pre_act, out_grad, w_up, w_down):
    gelu_value, gelu_slope = gelu_parts(pre_act.astype(jnp.float32))
    act = gelu_value.astype(jnp.bfloat16)
    hidden_grad = jnp.dot(out_grad, w_down.T, preferred_element_type=jnp.float32)
    pre_grad = (hidden_grad * gelu_slope).astype(jnp.bfloat16)
    in_grad = jnp.dot(pre_grad, w_up.T, preferred_element_type=jnp.float32).astype(jnp.bfloat16)
    total = jnp.dot(out_grad.T, act, preferred_element_type=jnp.float32)
    down_grad_t = total / math.sqrt(TOKENS)
    return (in_grad, down_grad_t)
```

```python
import math

import jax
import jax.numpy as jnp
from jax import lax
from jax.sharding import PartitionSpec as P

BF16 = jnp.bfloat16
F32 = jnp.float32


def gelu_value_of(pre):
    pre_float = pre.astype(F32)
    normal_cdf = 0.5 * (1.0 + jax.scipy.special.erf(pre_float / math.sqrt(2.0)))
    return (pre_float * normal_cdf).astype(BF16)


def gelu_slope_of(pre):
    pre_float = pre.astype(F32)
    normal_cdf = 0.5 * (1.0 + jax.scipy.special.erf(pre_float / math.sqrt(2.0)))
    density = jnp.exp(-0.5 * pre_float * pre_float) / math.sqrt(2.0 * math.pi)
    return normal_cdf + pre_float * density


def xor_permute(value, axis, mask):
    count = lax.axis_size(axis)
    return lax.ppermute(value, axis, [(i, i ^ mask) for i in range(count)])


def either(bit, low, high):
    return jnp.where(bit == 0, low, high)


def gathered_plan(pre_act, out_grad, w_up, w_down):
    act = gelu_value_of(pre_act)
    gathered = lax.all_gather(out_grad, "tensor", axis=0, tiled=True)
    hidden_grad = lax.dot_general(gathered, w_down, (((1,), (1,)), ((), ())), preferred_element_type=F32)
    pre_grad = (hidden_grad * gelu_slope_of(pre_act)).astype(BF16)
    all_tokens = gathered.shape[0] * lax.axis_size("dp")
    my_columns = lax.all_to_all(gathered, "dp", split_axis=1, concat_axis=0, tiled=True)
    summed = lax.dot_general(
        my_columns,
        lax.all_gather(act, "dp", axis=0, tiled=True),
        (((0,), (0,)), ((), ())),
        preferred_element_type=F32,
    )
    in_grad = lax.psum_scatter(
        lax.dot_general(pre_grad, w_up, (((1,), (1,)), ((), ())), preferred_element_type=F32),
        "tensor",
        scatter_dimension=0,
        tiled=True,
    ).astype(BF16)
    return (in_grad, summed / math.sqrt(all_tokens))


def plane_plan(pre_act, out_grad, w_up, w_down):
    place, shard = lax.axis_index("dp"), lax.axis_index("tensor")
    z, x = place // 2, place % 2
    y, core = shard // 2, shard % 2
    rows, width = out_grad.shape
    tokens, units = pre_act.shape
    half = units // 2
    pair = width // 4
    block = pair // 2
    scale = 1.0 / math.sqrt(tokens * 8)
    chunks = ((0, half // 2), (half // 2, half // 3), (half // 2 + half // 3, half // 6))

    def columns(bit, offset, size):
        low = pre_act[:, offset : offset + size]
        high = pre_act[:, half + offset : half + offset + size]
        return gelu_value_of(either(bit, low, high))

    kept = [columns(x, o, w) for o, w in chunks]
    sent = [columns(1 - x, o, w) for o, w in chunks]

    def spread(own):
        far = xor_permute(own, "dp", 4)
        near = xor_permute(own, "dp", 2)
        return [own, near, far, xor_permute(far, "dp", 2)]

    got0 = xor_permute(sent[0], "dp", 1)
    first_own = spread(kept[0])
    first_got = spread(got0)
    acts = [jnp.concatenate([p for pair_ in zip(first_own, first_got) for p in pair_])]
    for own, out in zip(kept[1:], sent[1:]):
        acts.append(jnp.concatenate(spread(jnp.concatenate([own, xor_permute(out, "dp", 1)]))))

    def slab(k):
        return lax.dynamic_slice(out_grad, (0, (z ^ k) * pair), (rows, pair))

    grad = jnp.stack([slab(0)] + [xor_permute(slab(k), "dp", 2 * k) for k in (1, 2, 3)])
    grad = jnp.stack([grad, xor_permute(grad, "dp", 1)], axis=1)
    other = xor_permute(grad, "tensor", 2)
    grad = jnp.stack([either(y, grad, other), either(y, other, grad)], axis=2)
    other = xor_permute(grad, "tensor", 1)
    grad = jnp.stack([either(core, grad, other), either(core, other, grad)], axis=3)
    grad = grad.reshape(8 * tokens, 2, block)
    mine, theirs = either(x, grad[:, 0], grad[:, 1]), either(x, grad[:, 1], grad[:, 0])
    both = jnp.concatenate([mine, theirs], axis=1)

    gathered = lax.all_gather(out_grad, "tensor", axis=0, tiled=True)
    hidden_grad = lax.dot_general(gathered, w_down, (((1,), (1,)), ((), ())), preferred_element_type=F32)
    pre_grad = (hidden_grad * gelu_slope_of(pre_act)).astype(BF16)
    partial = lax.dot_general(pre_grad, w_up, (((1,), (1,)), ((), ())), preferred_element_type=F32)
    partial = partial.reshape(2, 2, rows, width)
    keep = either(core, partial[:, 0], partial[:, 1])
    give = either(core, partial[:, 1], partial[:, 0])
    keep = keep + xor_permute(give, "tensor", 1)
    in_grad = either(y, keep[0], keep[1]) + xor_permute(either(y, keep[1], keep[0]), "tensor", 2)

    ours, back = [], []
    for act in acts:
        product = scale * lax.dot_general(both, act, (((0,), (0,)), ((), ())), preferred_element_type=F32)
        ours.append(product[:block])
        back.append(xor_permute(product[block:].astype(BF16), "dp", 1))
    ours = jnp.concatenate(ours, axis=1)
    back = jnp.concatenate(back, axis=1).astype(F32)
    down_grad_t = jnp.concatenate([either(x, ours, back), either(x, back, ours)], axis=1)
    return (in_grad.astype(BF16), down_grad_t)


def solution(mesh):
    plan = plane_plan if (mesh.shape["dp"], mesh.shape["tensor"]) == (8, 4) else gathered_plan
    placed = (P("dp", "tensor"), P(("dp", "tensor"), None), P(None, "tensor"), P("tensor", None))
    return jax.shard_map(
        plan,
        mesh=mesh,
        in_specs=placed,
        out_specs=(P(("dp", "tensor"), None), P("dp", "tensor")),
        check_vma=False,
    )
```

```python
import math

import jax
import jax.numpy as jnp
from jax import lax
from jax.experimental import pallas as pl
from jax.experimental.pallas import tpu as pltpu
from jax.sharding import PartitionSpec as P

BF16 = jnp.bfloat16
F32 = jnp.float32


def gelu_value_of(pre):
    pre_float = pre.astype(F32)
    normal_cdf = 0.5 * (1.0 + jax.scipy.special.erf(pre_float / math.sqrt(2.0)))
    return (pre_float * normal_cdf).astype(BF16)


def gelu_slope_of(pre):
    pre_float = pre.astype(F32)
    normal_cdf = 0.5 * (1.0 + jax.scipy.special.erf(pre_float / math.sqrt(2.0)))
    density = jnp.exp(-0.5 * pre_float * pre_float) / math.sqrt(2.0 * math.pi)
    return normal_cdf + pre_float * density


def xor_permute(value, axis, mask):
    count = lax.axis_size(axis)
    return lax.ppermute(value, axis, [(i, i ^ mask) for i in range(count)])


def either(bit, low, high):
    return jnp.where(bit == 0, low, high)


def gathered_plan(pre_act, out_grad, w_up, w_down):
    act = gelu_value_of(pre_act)
    gathered = lax.all_gather(out_grad, "tensor", axis=0, tiled=True)
    hidden_grad = lax.dot_general(gathered, w_down, (((1,), (1,)), ((), ())), preferred_element_type=F32)
    pre_grad = (hidden_grad * gelu_slope_of(pre_act)).astype(BF16)
    all_tokens = gathered.shape[0] * lax.axis_size("dp")
    my_columns = lax.all_to_all(gathered, "dp", split_axis=1, concat_axis=0, tiled=True)
    summed = lax.dot_general(
        my_columns,
        lax.all_gather(act, "dp", axis=0, tiled=True),
        (((0,), (0,)), ((), ())),
        preferred_element_type=F32,
    )
    in_grad = lax.psum_scatter(
        lax.dot_general(pre_grad, w_up, (((1,), (1,)), ((), ())), preferred_element_type=F32),
        "tensor",
        scatter_dimension=0,
        tiled=True,
    ).astype(BF16)
    return (in_grad, summed / math.sqrt(all_tokens))


VMEM_LIMIT = 48 * 1024 * 1024
NT = (((1,), (1,)), ((), ()))


def params():
    return pltpu.CompilerParams(vmem_limit_bytes=VMEM_LIMIT)


def cost(flops, moved):
    return pl.CostEstimate(flops=flops, bytes_accessed=moved, transcendentals=0)


def whole():
    return pl.BlockSpec(memory_space=pltpu.VMEM)


def weights_pass(place, own, got, slope, w_up, w_down, before, first, last, size):
    pairs, rows, width = own.shape
    tokens = 2 * pairs * rows
    start = first // size

    def body(place_ref, own_ref, got_ref, slope_ref, up_ref, down_ref, *rest):
        before_ref = rest[0] if before is not None else None
        total_ref, grad_ref = rest[-2:]

        @pl.when(pl.program_id(0) == 0)
        def _():
            shard = place_ref[1]
            for i in range(pairs):
                for ref, bit in ((own_ref, 0), (got_ref, 1)):
                    at = pl.multiple_of(((2 * i + bit) ^ shard) * rows, rows)
                    grad_ref[pl.ds(at, rows), :] = ref[i]
            total_ref[...] = jnp.zeros_like(total_ref) if before_ref is None else before_ref[...]

        hidden = lax.dot_general(grad_ref[...], down_ref[...], NT, preferred_element_type=F32)
        pre_grad = (hidden * slope_ref[...]).astype(BF16)
        total_ref[...] += lax.dot_general(pre_grad, up_ref[...], NT, preferred_element_type=F32)

    const2, const3 = (lambda i: (0, 0)), (lambda i: (0, 0, 0))
    specs = [
        pl.BlockSpec(memory_space=pltpu.SMEM),
        pl.BlockSpec(own.shape, const3),
        pl.BlockSpec(got.shape, const3),
        pl.BlockSpec((tokens, size), lambda i: (0, i + start)),
        pl.BlockSpec((width, size), lambda i: (0, i + start)),
        pl.BlockSpec((size, width), lambda i: (i + start, 0)),
    ]
    operands = [place, own, got, slope, w_up, w_down]
    if before is not None:
        specs.append(pl.BlockSpec((tokens, width), const2))
        operands.append(before)
    units = last - first
    return pl.pallas_call(
        body,
        grid=(units // size,),
        in_specs=specs,
        out_specs=pl.BlockSpec((tokens, width), const2),
        out_shape=jax.ShapeDtypeStruct((tokens, width), F32),
        scratch_shapes=[pltpu.VMEM((tokens, width), BF16)],
        compiler_params=params(),
        cost_estimate=cost(4 * tokens * units * width, 4 * units * width),
    )(*operands)


def prepare(place, own, got):
    _, _, depth, rows, pair = own.shape
    block = pair // 2
    tokens = 2 * depth * 4 * rows

    def body(place_ref, own_ref, got_ref, mine_ref, theirs_ref, held_ref):
        x, shard = place_ref[0], place_ref[1]
        for k in range(depth):
            for j in range(2):
                for i in range(2):
                    for ref, bit in ((own_ref, 0), (got_ref, 1)):
                        at = (2 * k + j) * 4 * rows + ((2 * i + bit) ^ shard) * rows
                        held_ref[pl.ds(pl.multiple_of(at, rows), rows), :] = ref[i, j, k]
        for out, bit in ((mine_ref, x), (theirs_ref, 1 - x)):
            columns = pl.ds(pl.multiple_of(bit * block, 128), block)
            out[...] = held_ref[:, columns].T

    shape = jax.ShapeDtypeStruct((block, tokens), BF16)
    return pl.pallas_call(
        body,
        in_specs=[pl.BlockSpec(memory_space=pltpu.SMEM), whole(), whole()],
        out_specs=[whole(), whole()],
        out_shape=[shape, shape],
        scratch_shapes=[pltpu.VMEM((tokens, pair), BF16)],
        compiler_params=params(),
        cost_estimate=cost(0, 8 * tokens * pair),
    )(place, own, got)


def contract(grad_ref, refs, scale):
    total, at = None, 0
    for ref in refs:
        depth = ref.shape[0]
        part = jnp.dot(grad_ref[:, at : at + depth], ref[...], preferred_element_type=F32)
        total = part if total is None else total + part
        at += depth
    return total * scale


def their_product(theirs, pieces, scale):
    def body(grad_ref, *refs):
        refs[-1][...] = contract(grad_ref, refs[:-1], scale).astype(BF16)

    block, tokens = theirs.shape
    size = pieces[0].shape[1]
    return pl.pallas_call(
        body,
        in_specs=[whole()] * (1 + len(pieces)),
        out_specs=whole(),
        out_shape=jax.ShapeDtypeStruct((block, size), BF16),
        compiler_params=params(),
        cost_estimate=cost(2 * block * tokens * size, 4 * tokens * size),
    )(theirs, *pieces)


def my_product(place, mine, chunks, backs, width, scale):
    block, tokens = mine.shape
    counts = [len(pieces) for pieces in chunks]
    sizes = [pieces[0].shape[1] for pieces in chunks]
    half = sum(sizes)

    def body(place_ref, grad_ref, *refs):
        pieces, returned = refs[: sum(counts)], refs[sum(counts) : sum(counts) + len(backs)]
        out_ref, held_ref, sems = refs[sum(counts) + len(backs) :]
        copies = []

        def store(slot, offset, size, side, value):
            here = held_ref.at[:, pl.ds(side * half + offset, size)]
            here[...] = value
            bit = place_ref[0] if side == 0 else 1 - place_ref[0]
            to = pl.ds(pl.multiple_of(bit * half + offset, 128), size)
            copies.append(pltpu.make_async_copy(here, out_ref.at[:, to], sems.at[slot]))
            copies[-1].start()

        offset = 0
        for slot, (ref, size) in enumerate(zip(returned, sizes)):
            store(slot, offset, size, 1, ref[...].astype(F32))
            offset += size
        offset = at = 0
        for slot, (count, size) in enumerate(zip(counts, sizes)):
            store(len(backs) + slot, offset, size, 0, contract(grad_ref, pieces[at : at + count], scale))
            offset, at = offset + size, at + count
        for copy in copies:
            copy.wait()

    flat = [p for pieces in chunks for p in pieces]
    return pl.pallas_call(
        body,
        in_specs=[pl.BlockSpec(memory_space=pltpu.SMEM)] + [whole()] * (1 + len(flat) + len(backs)),
        out_specs=pl.BlockSpec(memory_space=pl.ANY),
        out_shape=jax.ShapeDtypeStruct((block, width), F32),
        scratch_shapes=[pltpu.VMEM((block, width), F32), pltpu.SemaphoreType.DMA((len(backs) + len(chunks),))],
        compiler_params=params(),
        cost_estimate=cost(2 * block * tokens * half, 4 * block * width),
    )(place, mine, *flat, *backs)


def place_back(place, result, back, offset):
    block, width = result.shape
    size = back.shape[1]

    def body(place_ref, back_ref, _, out_ref, held_ref, sem):
        held_ref[...] = back_ref[...].astype(F32)
        to = pl.ds(pl.multiple_of((1 - place_ref[0]) * (width // 2) + offset, 128), size)
        copy = pltpu.make_async_copy(held_ref, out_ref.at[:, to], sem)
        copy.start()
        copy.wait()

    return pl.pallas_call(
        body,
        in_specs=[pl.BlockSpec(memory_space=pltpu.SMEM), whole(), pl.BlockSpec(memory_space=pl.ANY)],
        out_specs=pl.BlockSpec(memory_space=pl.ANY),
        out_shape=jax.ShapeDtypeStruct(result.shape, F32),
        input_output_aliases={2: 0},
        scratch_shapes=[pltpu.VMEM((block, size), F32), pltpu.SemaphoreType.DMA],
        compiler_params=params(),
        cost_estimate=cost(0, 4 * block * size),
    )(place, back, result)


def after(value, *others):
    return lax.optimization_barrier((value, *others))[0]


def plane_plan(pre_act, out_grad, w_up, w_down):
    at, shard = lax.axis_index("dp"), lax.axis_index("tensor")
    z, x = at // 2, at % 2
    y, core = shard // 2, shard % 2
    place = jnp.stack([x, shard]).astype(jnp.int32)
    rows, width = out_grad.shape
    tokens, units = pre_act.shape
    half = units // 2
    pair = width // 4
    scale = 1.0 / math.sqrt(tokens * 8)
    chunks = ((0, half // 2), (half // 2, half // 3), (half // 2 + half // 3, half // 6))

    def columns(pre, bit, offset, size):
        low = pre[:, offset : offset + size]
        high = pre[:, half + offset : half + offset + size]
        return gelu_value_of(either(bit, low, high))

    def slab(k):
        return lax.dynamic_slice(out_grad, (0, (z ^ k) * pair), (rows, pair))

    grad = jnp.stack([slab(0)] + [xor_permute(slab(k), "dp", 2 * k) for k in (1, 2, 3)])

    kept0, sent0 = columns(pre_act, x, *chunks[0]), columns(pre_act, 1 - x, *chunks[0])

    got0 = xor_permute(sent0, "dp", 1)
    far_own = xor_permute(kept0, "dp", 4)
    later_act, later_kept0, later_grad, grad = lax.optimization_barrier((pre_act, kept0, out_grad, grad))
    near_own = xor_permute(later_kept0, "dp", 2)
    own_rows = xor_permute(later_grad, "tensor", 2)
    grad_x = xor_permute(grad, "dp", 1)
    slope = gelu_slope_of(later_act)
    kept = [columns(later_act, x, o, w) for o, w in chunks[1:]]
    sent = [columns(later_act, 1 - x, o, w) for o, w in chunks[1:]]

    group = jnp.stack([out_grad, own_rows])
    group_got = xor_permute(group, "tensor", 1)
    far_got = xor_permute(got0, "dp", 4)
    near_got = xor_permute(got0, "dp", 2)
    both_x = jnp.stack([grad, grad_x])
    grad_y = xor_permute(both_x, "tensor", 2)
    got1 = xor_permute(after(sent[0], grad_x), "dp", 1)
    last_own = xor_permute(far_own, "dp", 2)

    size = 256
    quarter = units // 4

    def weights(part, before, *waits):
        if before is None:
            first_group = after(group, *waits)
        else:
            first_group, before = group, after(before, *waits)
        return weights_pass(
            place, first_group, group_got, slope, w_up, w_down, before, part * quarter, (part + 1) * quarter, size
        )

    partial = weights(0, None, slope, far_own, near_own)
    got2 = xor_permute(after(sent[1], got1), "dp", 1)
    partial = weights(1, partial, grad_y, got1)
    both_y = jnp.stack([both_x, grad_y])
    grad_core = xor_permute(both_y, "tensor", 1)
    own1 = jnp.concatenate([kept[0], got1])
    far1 = xor_permute(after(own1, near_got), "dp", 4)
    last_got = xor_permute(far_got, "dp", 2)
    partial = weights(2, partial, far_got, near_got, got2)
    near1 = xor_permute(after(own1, last_own), "dp", 2)
    partial = weights(3, partial, last_own)
    mine, theirs = prepare(place, both_y, after(grad_core, partial))
    own2 = after(jnp.concatenate([kept[1], got2]), last_got)
    far2 = xor_permute(own2, "dp", 4)
    last1 = xor_permute(far1, "dp", 2)
    near2 = xor_permute(after(own2, near1), "dp", 2)
    last2 = xor_permute(far2, "dp", 2)
    acts = [
        [kept0, got0, near_own, near_got, far_own, far_got, last_own, last_got],
        [own1, near1, far1, last1],
        [own2, near2, far2, last2],
    ]

    partial = partial.reshape(2, 2, rows, width)
    keep = either(core, partial[:, 0], partial[:, 1])
    give = either(core, partial[:, 1], partial[:, 0])
    keep = keep + xor_permute(give, "tensor", 1)
    in_grad = either(y, keep[0], keep[1]) + xor_permute(either(y, keep[1], keep[0]), "tensor", 2)

    backs = [xor_permute(their_product(theirs, pieces, scale), "dp", 1) for pieces in acts]
    result = my_product(place, mine, acts, backs[:-1], units, scale)
    result = place_back(place, result, backs[-1], chunks[-1][0])
    return (in_grad.astype(BF16), result)


def solution(mesh):
    plan = plane_plan if (mesh.shape["dp"], mesh.shape["tensor"]) == (8, 4) else gathered_plan
    placed = (P("dp", "tensor"), P(("dp", "tensor"), None), P(None, "tensor"), P("tensor", None))
    return jax.shard_map(
        plan,
        mesh=mesh,
        in_specs=placed,
        out_specs=(P(("dp", "tensor"), None), P("dp", "tensor")),
        check_vma=False,
    )
```

```python
import math

import jax
import jax.numpy as jnp
from jax import lax
from jax.experimental import pallas as pl
from jax.experimental.pallas import tpu as pltpu
from jax.sharding import PartitionSpec as P

BF16 = jnp.bfloat16
F32 = jnp.float32


def gelu_value_of(pre):
    pre_float = pre.astype(F32)
    normal_cdf = 0.5 * (1.0 + jax.scipy.special.erf(pre_float / math.sqrt(2.0)))
    return (pre_float * normal_cdf).astype(BF16)


def gelu_slope_of(pre):
    pre_float = pre.astype(F32)
    normal_cdf = 0.5 * (1.0 + jax.scipy.special.erf(pre_float / math.sqrt(2.0)))
    density = jnp.exp(-0.5 * pre_float * pre_float) / math.sqrt(2.0 * math.pi)
    return normal_cdf + pre_float * density


def xor_permute(value, axis, mask):
    count = lax.axis_size(axis)
    return lax.ppermute(value, axis, [(i, i ^ mask) for i in range(count)])


def either(bit, low, high):
    return jnp.where(bit == 0, low, high)


def gathered_plan(pre_act, out_grad, w_up, w_down):
    act = gelu_value_of(pre_act)
    gathered = lax.all_gather(out_grad, "tensor", axis=0, tiled=True)
    hidden_grad = lax.dot_general(gathered, w_down, (((1,), (1,)), ((), ())), preferred_element_type=F32)
    pre_grad = (hidden_grad * gelu_slope_of(pre_act)).astype(BF16)
    all_tokens = gathered.shape[0] * lax.axis_size("dp")
    my_columns = lax.all_to_all(gathered, "dp", split_axis=1, concat_axis=0, tiled=True)
    summed = lax.dot_general(
        my_columns,
        lax.all_gather(act, "dp", axis=0, tiled=True),
        (((0,), (0,)), ((), ())),
        preferred_element_type=F32,
    )
    in_grad = lax.psum_scatter(
        lax.dot_general(pre_grad, w_up, (((1,), (1,)), ((), ())), preferred_element_type=F32),
        "tensor",
        scatter_dimension=0,
        tiled=True,
    ).astype(BF16)
    return (in_grad, summed / math.sqrt(all_tokens))


VMEM_LIMIT = 16 * 1024 * 1024


def params():
    return pltpu.CompilerParams(vmem_limit_bytes=VMEM_LIMIT)


def cost(flops, moved):
    return pl.CostEstimate(flops=flops, bytes_accessed=moved, transcendentals=0)


def whole():
    return pl.BlockSpec(memory_space=pltpu.VMEM)


def prepare(place, own, got):
    _, _, depth, rows, pair = own.shape
    block = pair // 2
    tokens = 2 * depth * 4 * rows

    def body(place_ref, own_ref, got_ref, mine_ref, theirs_ref, held_ref):
        x, shard = place_ref[0], place_ref[1]
        for k in range(depth):
            for j in range(2):
                for i in range(2):
                    for ref, bit in ((own_ref, 0), (got_ref, 1)):
                        at = (2 * k + j) * 4 * rows + ((2 * i + bit) ^ shard) * rows
                        held_ref[pl.ds(pl.multiple_of(at, rows), rows), :] = ref[i, j, k]
        for out, bit in ((mine_ref, x), (theirs_ref, 1 - x)):
            columns = pl.ds(pl.multiple_of(bit * block, 128), block)
            out[...] = held_ref[:, columns].T

    shape = jax.ShapeDtypeStruct((block, tokens), BF16)
    return pl.pallas_call(
        body,
        in_specs=[pl.BlockSpec(memory_space=pltpu.SMEM), whole(), whole()],
        out_specs=[whole(), whole()],
        out_shape=[shape, shape],
        scratch_shapes=[pltpu.VMEM((tokens, pair), BF16)],
        compiler_params=params(),
        cost_estimate=cost(0, 8 * tokens * pair),
    )(place, own, got)


def contract(grad_ref, refs, scale):
    total, at = None, 0
    for ref in refs:
        depth = ref.shape[0]
        part = jnp.dot(grad_ref[:, at : at + depth], ref[...], preferred_element_type=F32)
        total = part if total is None else total + part
        at += depth
    return total * scale


def their_product(theirs, shared, last, chunk, scale):
    def body(grad_ref, *refs):
        refs[-1][...] = contract(grad_ref, refs[:-1], scale).astype(BF16)

    block, tokens = theirs.shape
    offset, size = chunk
    specs = [pl.BlockSpec(p.shape[:1] + (size,), lambda i: (0, offset // size)) for p in shared]
    return pl.pallas_call(
        body,
        grid=(1,),
        in_specs=[pl.BlockSpec(theirs.shape, lambda i: (0, 0))]
        + specs
        + [pl.BlockSpec(last.shape, lambda i: (0, 0))],
        out_specs=pl.BlockSpec((block, size), lambda i: (0, 0)),
        out_shape=jax.ShapeDtypeStruct((block, size), BF16),
        compiler_params=params(),
        cost_estimate=cost(2 * block * tokens * size, 4 * tokens * size),
    )(theirs, *shared, last)


def my_product(place, mine, shared, lasts, chunks, backs, width, scale):
    block, tokens = mine.shape
    half = width // 2
    count = len(chunks)

    def body(place_ref, grad_ref, *refs):
        shared_refs, refs = refs[: len(shared)], refs[len(shared) :]
        last_refs, returned = refs[:count], refs[count : count + len(backs)]
        out_ref, held_ref, sems = refs[count + len(backs) :]
        copies = []

        def store(slot, offset, size, side, value):
            here = held_ref.at[:, pl.ds(side * half + offset, size)]
            here[...] = value
            bit = place_ref[0] if side == 0 else 1 - place_ref[0]
            to = pl.ds(pl.multiple_of(bit * half + offset, 128), size)
            copies.append(pltpu.make_async_copy(here, out_ref.at[:, to], sems.at[slot]))
            copies[-1].start()

        for slot, (ref, (offset, size)) in enumerate(zip(returned, chunks)):
            store(slot, offset, size, 1, ref[...].astype(F32))
        for slot, (ref, (offset, size)) in enumerate(zip(last_refs, chunks)):
            pieces = [r.at[:, pl.ds(offset, size)] for r in shared_refs] + [ref]
            store(len(backs) + slot, offset, size, 0, contract(grad_ref, pieces, scale))
        for copy in copies:
            copy.wait()

    return pl.pallas_call(
        body,
        in_specs=[pl.BlockSpec(memory_space=pltpu.SMEM)] + [whole()] * (1 + len(shared) + count + len(backs)),
        out_specs=pl.BlockSpec(memory_space=pl.ANY),
        out_shape=jax.ShapeDtypeStruct((block, width), F32),
        scratch_shapes=[pltpu.VMEM((block, width), F32), pltpu.SemaphoreType.DMA((len(backs) + count,))],
        compiler_params=params(),
        cost_estimate=cost(2 * block * tokens * half, 4 * block * width),
    )(place, mine, *shared, *lasts, *backs)


def place_back(place, result, back, offset):
    block, width = result.shape
    size = back.shape[1]

    def body(place_ref, back_ref, _, out_ref, held_ref, sem):
        held_ref[...] = back_ref[...].astype(F32)
        to = pl.ds(pl.multiple_of((1 - place_ref[0]) * (width // 2) + offset, 128), size)
        copy = pltpu.make_async_copy(held_ref, out_ref.at[:, to], sem)
        copy.start()
        copy.wait()

    return pl.pallas_call(
        body,
        in_specs=[pl.BlockSpec(memory_space=pltpu.SMEM), whole(), pl.BlockSpec(memory_space=pl.ANY)],
        out_specs=pl.BlockSpec(memory_space=pl.ANY),
        out_shape=jax.ShapeDtypeStruct(result.shape, F32),
        input_output_aliases={2: 0},
        scratch_shapes=[pltpu.VMEM((block, size), F32), pltpu.SemaphoreType.DMA],
        compiler_params=params(),
        cost_estimate=cost(0, 4 * block * size),
    )(place, back, result)


def after(value, *others):
    return lax.optimization_barrier((value, *others))[0]


def plane_plan(pre_act, out_grad, w_up, w_down):
    at, shard = lax.axis_index("dp"), lax.axis_index("tensor")
    z, x = at // 2, at % 2
    y, core = shard // 2, shard % 2
    place = jnp.stack([x, shard]).astype(jnp.int32)
    rows, width = out_grad.shape
    tokens, units = pre_act.shape
    half = units // 2
    pair = width // 4
    scale = 1.0 / math.sqrt(tokens * 8)
    chunks = tuple((i * half // 3, half // 3) for i in range(3))

    def columns(pre, bit):
        return gelu_value_of(either(bit, pre[:, :half], pre[:, half:]))

    def slab(k):
        return lax.dynamic_slice(out_grad, (0, (z ^ k) * pair), (rows, pair))

    grad = jnp.stack([slab(0)] + [xor_permute(slab(k), "dp", 2 * k) for k in (1, 2, 3)])

    kept, sent = columns(pre_act, x), columns(pre_act, 1 - x)
    grad = after(grad, kept, sent)
    far_own = xor_permute(kept, "dp", 4)
    near_own = xor_permute(kept, "dp", 2)
    grad_x = xor_permute(grad, "dp", 1)
    got = xor_permute(after(sent, grad), "dp", 1)
    far_got = xor_permute(got, "dp", 4)
    near_got = xor_permute(got, "dp", 2)

    both_x = jnp.stack([grad, grad_x])
    grad_y = xor_permute(both_x, "tensor", 2)

    other = xor_permute(out_grad, "tensor", 2)
    rows_y = jnp.stack([either(y, out_grad, other), either(y, other, out_grad)])
    other = xor_permute(rows_y, "tensor", 1)
    group = jnp.stack([either(core, rows_y, other), either(core, other, rows_y)], axis=1).reshape(tokens, width)
    group = after(group, got, grad_x)
    hidden_grad = lax.dot_general(group, w_down, (((1,), (1,)), ((), ())), preferred_element_type=F32)
    pre_grad = (hidden_grad * gelu_slope_of(pre_act)).astype(BF16)
    partial = lax.dot_general(pre_grad, w_up, (((1,), (1,)), ((), ())), preferred_element_type=F32)

    far_own, far_got, near_own, near_got, grad_y = lax.optimization_barrier(
        (far_own, far_got, near_own, near_got, grad_y, partial)
    )[:5]
    both_y = jnp.stack([both_x, grad_y])
    grad_core = xor_permute(both_y, "tensor", 1)
    lasts = []
    for offset, size in chunks:
        far = jnp.concatenate([far_own[:, offset : offset + size], far_got[:, offset : offset + size]])
        lasts.append(xor_permute(far, "dp", 2))
    mine, theirs = prepare(place, both_y, grad_core)
    shared = [kept, got, near_own, near_got, far_own, far_got]
    backs = [xor_permute(their_product(theirs, shared, f, c, scale), "dp", 1) for f, c in zip(lasts, chunks)]

    partial = after(partial, grad_core).reshape(2, 2, rows, width)
    keep = either(core, partial[:, 0], partial[:, 1])
    give = either(core, partial[:, 1], partial[:, 0])
    keep = keep + xor_permute(give, "tensor", 1)
    in_grad = either(y, keep[0], keep[1]) + xor_permute(either(y, keep[1], keep[0]), "tensor", 2)

    result = my_product(place, mine, shared, lasts, chunks, backs[:-1], units, scale)
    result = place_back(place, result, backs[-1], chunks[-1][0])
    return (in_grad.astype(BF16), result)


def solution(mesh):
    plan = plane_plan if (mesh.shape["dp"], mesh.shape["tensor"]) == (8, 4) else gathered_plan
    placed = (P("dp", "tensor"), P(("dp", "tensor"), None), P(None, "tensor"), P("tensor", None))
    return jax.shard_map(
        plan,
        mesh=mesh,
        in_specs=placed,
        out_specs=(P(("dp", "tensor"), None), P("dp", "tensor")),
        check_vma=False,
    )
```

```python
import math

import jax
import jax.numpy as jnp
from jax import lax
from jax.experimental import pallas as pl
from jax.experimental.pallas import tpu as pltpu
from jax.sharding import PartitionSpec as P

BF16 = jnp.bfloat16
F32 = jnp.float32


def gelu_value_of(pre):
    pre_float = pre.astype(F32)
    normal_cdf = 0.5 * (1.0 + jax.scipy.special.erf(pre_float / math.sqrt(2.0)))
    return (pre_float * normal_cdf).astype(BF16)


def gelu_slope_of(pre):
    pre_float = pre.astype(F32)
    normal_cdf = 0.5 * (1.0 + jax.scipy.special.erf(pre_float / math.sqrt(2.0)))
    density = jnp.exp(-0.5 * pre_float * pre_float) / math.sqrt(2.0 * math.pi)
    return normal_cdf + pre_float * density


def xor_permute(value, axis, mask):
    count = lax.axis_size(axis)
    return lax.ppermute(value, axis, [(i, i ^ mask) for i in range(count)])


def either(bit, low, high):
    return jnp.where(bit == 0, low, high)


def gathered_plan(pre_act, out_grad, w_up, w_down):
    act = gelu_value_of(pre_act)
    gathered = lax.all_gather(out_grad, "tensor", axis=0, tiled=True)
    hidden_grad = lax.dot_general(gathered, w_down, (((1,), (1,)), ((), ())), preferred_element_type=F32)
    pre_grad = (hidden_grad * gelu_slope_of(pre_act)).astype(BF16)
    all_tokens = gathered.shape[0] * lax.axis_size("dp")
    my_columns = lax.all_to_all(gathered, "dp", split_axis=1, concat_axis=0, tiled=True)
    summed = lax.dot_general(
        my_columns,
        lax.all_gather(act, "dp", axis=0, tiled=True),
        (((0,), (0,)), ((), ())),
        preferred_element_type=F32,
    )
    in_grad = lax.psum_scatter(
        lax.dot_general(pre_grad, w_up, (((1,), (1,)), ((), ())), preferred_element_type=F32),
        "tensor",
        scatter_dimension=0,
        tiled=True,
    ).astype(BF16)
    return (in_grad, summed / math.sqrt(all_tokens))


VMEM_LIMIT = 16 * 1024 * 1024


def params():
    return pltpu.CompilerParams(vmem_limit_bytes=VMEM_LIMIT)


def cost(flops, moved):
    return pl.CostEstimate(flops=flops, bytes_accessed=moved, transcendentals=0)


def whole():
    return pl.BlockSpec(memory_space=pltpu.VMEM)


def prepare(place, blocks):
    _, depth, rows, pair = blocks[0].shape
    block = pair // 2
    tokens = 2 * depth * len(blocks) * rows

    def body(place_ref, *refs):
        mine_ref, theirs_ref, held_ref = refs[len(blocks) :]
        x, shard = place_ref[0], place_ref[1]
        for i, ref in enumerate(refs[: len(blocks)]):
            for k in range(depth):
                for j in range(2):
                    at = ((2 * (k % 2 * 2 + k // 2) + j) * len(blocks) + (i ^ shard)) * rows
                    held_ref[pl.ds(pl.multiple_of(at, rows), rows), :] = ref[j, k]
        for out, bit in ((mine_ref, x), (theirs_ref, 1 - x)):
            columns = pl.ds(pl.multiple_of(bit * block, 128), block)
            out[...] = held_ref[:, columns].T

    shape = jax.ShapeDtypeStruct((block, tokens), BF16)
    return pl.pallas_call(
        body,
        in_specs=[pl.BlockSpec(memory_space=pltpu.SMEM)] + [whole()] * len(blocks),
        out_specs=[whole(), whole()],
        out_shape=[shape, shape],
        scratch_shapes=[pltpu.VMEM((tokens, pair), BF16)],
        compiler_params=params(),
        cost_estimate=cost(0, 8 * tokens * pair),
    )(place, *blocks)


def contract(grad_ref, refs, pieces, scale):
    total, row = None, 0
    for ref, (piece, offset, size) in zip(refs, pieces):
        depth = piece.shape[0]
        value = ref[:, offset : offset + size]
        part = jnp.dot(grad_ref[:, row : row + depth], value, preferred_element_type=F32)
        total = part if total is None else total + part
        row += depth
    return total * scale


def their_product(theirs, pieces, scale):
    def body(grad_ref, *refs):
        refs[-1][...] = contract(grad_ref, refs[:-1], pieces, scale).astype(BF16)

    block, tokens = theirs.shape
    size = pieces[0][2]
    return pl.pallas_call(
        body,
        in_specs=[whole()] * (1 + len(pieces)),
        out_specs=whole(),
        out_shape=jax.ShapeDtypeStruct((block, size), BF16),
        compiler_params=params(),
        cost_estimate=cost(2 * block * tokens * size, 4 * tokens * size),
    )(theirs, *[piece for piece, _, _ in pieces])


def write_columns(place, result, mine, products, backs, width, scale):
    block, tokens = mine.shape
    half = width // 2
    flat = [piece for pieces, _ in products for piece, _, _ in pieces]
    sizes = [pieces[0][2] for pieces, _ in products] + [back.shape[1] for back, _ in backs]
    first = 0 if result is None else 1

    def body(place_ref, grad_ref, *refs):
        refs = refs[first:]
        piece_refs, back_refs = refs[: len(flat)], refs[len(flat) : len(flat) + len(backs)]
        out_ref, held_ref, sems = refs[len(flat) + len(backs) :]
        copies = []

        def store(bit, column, size, value):
            slot = len(copies)
            here = held_ref.at[:, pl.ds(sum(sizes[:slot]), size)]
            here[...] = value
            to = pl.ds(pl.multiple_of(bit * half + column, 128), size)
            copies.append(pltpu.make_async_copy(here, out_ref.at[:, to], sems.at[slot]))
            copies[-1].start()

        at = 0
        for pieces, column in products:
            value = contract(grad_ref, piece_refs[at : at + len(pieces)], pieces, scale)
            store(place_ref[0], column, pieces[0][2], value)
            at += len(pieces)
        for ref, (back, column) in zip(back_refs, backs):
            store(1 - place_ref[0], column, back.shape[1], ref[...].astype(F32))
        for copy in copies:
            copy.wait()

    held = [] if result is None else [result]
    return pl.pallas_call(
        body,
        in_specs=[pl.BlockSpec(memory_space=pltpu.SMEM), whole() if products else pl.BlockSpec(memory_space=pl.ANY)]
        + [pl.BlockSpec(memory_space=pl.ANY)] * first
        + [whole()] * (len(flat) + len(backs)),
        out_specs=pl.BlockSpec(memory_space=pl.ANY),
        out_shape=jax.ShapeDtypeStruct((block, width), F32),
        input_output_aliases={2: 0} if first else {},
        scratch_shapes=[pltpu.VMEM((block, sum(sizes)), F32), pltpu.SemaphoreType.DMA((len(sizes),))],
        compiler_params=params(),
        cost_estimate=cost(2 * block * tokens * sum(sizes) if products else 0, 4 * block * sum(sizes)),
    )(place, mine, *held, *flat, *[back for back, _ in backs])


def after(value, *others):
    return lax.optimization_barrier((value, *others))[0]


def plane_plan(pre_act, out_grad, w_up, w_down):
    at, shard = lax.axis_index("dp"), lax.axis_index("tensor")
    z, x = at // 2, at % 2
    y, core = shard // 2, shard % 2
    place = jnp.stack([x, shard]).astype(jnp.int32)
    rows, width = out_grad.shape
    tokens, units = pre_act.shape
    half = units // 2
    pair = width // 4
    scale = 1.0 / math.sqrt(tokens * 8)
    head = half // 3
    tail = half // 4
    middle = half - head - tail

    def columns(pre, bit, offset, size):
        low = pre[:, offset : offset + size]
        high = pre[:, half + offset : half + offset + size]
        return gelu_value_of(either(bit, low, high))

    kept0, sent0 = columns(pre_act, x, 0, head), columns(pre_act, 1 - x, 0, head)
    got0 = xor_permute(sent0, "dp", 1)
    later_act = after(pre_act, sent0)
    kept, sent = columns(later_act, x, head, half - head), columns(later_act, 1 - x, head, half - head)
    got = xor_permute(sent, "dp", 1)
    own0 = jnp.concatenate([kept0, got0])
    far0 = xor_permute(own0, "dp", 4)
    near0 = xor_permute(own0, "dp", 2)

    other = xor_permute(out_grad, "tensor", 2)
    rows_y = jnp.stack([either(y, out_grad, other), either(y, other, out_grad)])
    other = xor_permute(rows_y, "tensor", 1)
    group = jnp.stack([either(core, rows_y, other), either(core, other, rows_y)], axis=1).reshape(tokens, width)

    later_grad = after(out_grad, own0)

    def slab(k):
        return lax.dynamic_slice(later_grad, (0, (z ^ k) * pair), (rows, pair))

    grad = jnp.stack([slab(0)] + [xor_permute(slab(k), "dp", 2 * k) for k in (1, 2, 3)])
    grad_x = xor_permute(grad, "dp", 1)
    both_x = jnp.stack([grad, grad_x])
    grads = [xor_permute(both_x, "tensor", i) for i in (1, 2, 3)]

    own = jnp.concatenate([kept, got])
    joint = xor_permute(after(jnp.concatenate([far0, own[:, :middle]], axis=1), near0), "dp", 2)
    far = xor_permute(after(own, far0, near0), "dp", 4)

    group = after(group, own, grad_x, far0, near0)
    hidden_grad = lax.dot_general(group, w_down, (((1,), (1,)), ((), ())), preferred_element_type=F32)
    pre_grad = (hidden_grad * gelu_slope_of(pre_act)).astype(BF16)
    partial = lax.dot_general(pre_grad, w_up, (((1,), (1,)), ((), ())), preferred_element_type=F32)

    joint, *grads = lax.optimization_barrier((joint, *grads, partial))[:-1]
    mine, theirs = prepare(place, [both_x, *grads])
    pieces0 = [(p, 0, head) for p in (own0, far0, near0, joint)]
    their0 = their_product(theirs, pieces0, scale)
    back0 = xor_permute(their0, "dp", 1)
    far = after(far, their0)
    last = xor_permute(far[:, :middle], "dp", 2)
    pieces1 = [(own, 0, middle), (far, 0, middle), (joint, head, middle), (last, 0, middle)]
    their1 = their_product(theirs, pieces1, scale)
    back1 = xor_permute(their1, "dp", 1)
    ends = xor_permute(jnp.concatenate([own[:, middle:], far[:, middle:]]), "dp", 2)
    pieces2 = [(own, middle, tail), (far, middle, tail), (ends, 0, tail)]
    their2 = their_product(theirs, pieces2, scale)
    back2 = xor_permute(their2, "dp", 1)
    products = [(pieces0, 0), (pieces1, head), (pieces2, head + middle)]
    backs = [(back0, 0), (back1, head), (back2, head + middle)]

    partial = after(partial, their0).reshape(2, 2, rows, width)
    keep = either(core, partial[:, 0], partial[:, 1])
    give = either(core, partial[:, 1], partial[:, 0])
    keep = keep + xor_permute(give, "tensor", 1)
    in_grad = either(y, keep[0], keep[1]) + xor_permute(either(y, keep[1], keep[0]), "tensor", 2)

    result = write_columns(place, None, after(mine, their2), products, backs[:1], units, scale)
    result = write_columns(place, result, mine, [], backs[1:2], units, scale)
    result = write_columns(place, result, mine, [], backs[2:], units, scale)
    return (in_grad.astype(BF16), result)


def solution(mesh):
    plan = plane_plan if (mesh.shape["dp"], mesh.shape["tensor"]) == (8, 4) else gathered_plan
    placed = (P("dp", "tensor"), P(("dp", "tensor"), None), P(None, "tensor"), P("tensor", None))
    return jax.shard_map(
        plan,
        mesh=mesh,
        in_specs=placed,
        out_specs=(P(("dp", "tensor"), None), P("dp", "tensor")),
        check_vma=False,
    )
```

```python
import math

import jax
import jax.numpy as jnp
from jax import lax
from jax.experimental import pallas as pl
from jax.experimental.pallas import tpu as pltpu
from jax.sharding import PartitionSpec as P

BF16 = jnp.bfloat16
F32 = jnp.float32


def gelu_value_of(pre):
    pre_float = pre.astype(F32)
    normal_cdf = 0.5 * (1.0 + jax.scipy.special.erf(pre_float / math.sqrt(2.0)))
    return (pre_float * normal_cdf).astype(BF16)


def gelu_slope_of(pre):
    pre_float = pre.astype(F32)
    normal_cdf = 0.5 * (1.0 + jax.scipy.special.erf(pre_float / math.sqrt(2.0)))
    density = jnp.exp(-0.5 * pre_float * pre_float) / math.sqrt(2.0 * math.pi)
    return normal_cdf + pre_float * density


def xor_permute(value, axis, mask):
    count = lax.axis_size(axis)
    return lax.ppermute(value, axis, [(i, i ^ mask) for i in range(count)])


def either(bit, low, high):
    return jnp.where(bit == 0, low, high)


def gathered_plan(pre_act, out_grad, w_up, w_down):
    act = gelu_value_of(pre_act)
    gathered = lax.all_gather(out_grad, "tensor", axis=0, tiled=True)
    hidden_grad = lax.dot_general(gathered, w_down, (((1,), (1,)), ((), ())), preferred_element_type=F32)
    pre_grad = (hidden_grad * gelu_slope_of(pre_act)).astype(BF16)
    all_tokens = gathered.shape[0] * lax.axis_size("dp")
    my_columns = lax.all_to_all(gathered, "dp", split_axis=1, concat_axis=0, tiled=True)
    summed = lax.dot_general(
        my_columns,
        lax.all_gather(act, "dp", axis=0, tiled=True),
        (((0,), (0,)), ((), ())),
        preferred_element_type=F32,
    )
    in_grad = lax.psum_scatter(
        lax.dot_general(pre_grad, w_up, (((1,), (1,)), ((), ())), preferred_element_type=F32),
        "tensor",
        scatter_dimension=0,
        tiled=True,
    ).astype(BF16)
    return (in_grad, summed / math.sqrt(all_tokens))


VMEM_LIMIT = 16 * 1024 * 1024


def params():
    return pltpu.CompilerParams(vmem_limit_bytes=VMEM_LIMIT)


def cost(flops, moved):
    return pl.CostEstimate(flops=flops, bytes_accessed=moved, transcendentals=0)


def whole():
    return pl.BlockSpec(memory_space=pltpu.VMEM)


def prepare(place, blocks):
    _, depth, rows, pair = blocks[0].shape
    block = pair // 2
    tokens = 2 * depth * len(blocks) * rows

    def body(place_ref, *refs):
        mine_ref, theirs_ref, held_ref = refs[len(blocks) :]
        x, shard = place_ref[0], place_ref[1]
        for i, ref in enumerate(refs[: len(blocks)]):
            for k in range(depth):
                for j in range(2):
                    at = ((2 * (k % 2 * 2 + k // 2) + j) * len(blocks) + (i ^ shard)) * rows
                    held_ref[pl.ds(pl.multiple_of(at, rows), rows), :] = ref[j, k]
        for out, bit in ((mine_ref, x), (theirs_ref, 1 - x)):
            columns = pl.ds(pl.multiple_of(bit * block, 128), block)
            out[...] = held_ref[:, columns].T

    shape = jax.ShapeDtypeStruct((block, tokens), BF16)
    return pl.pallas_call(
        body,
        in_specs=[pl.BlockSpec(memory_space=pltpu.SMEM)] + [whole()] * len(blocks),
        out_specs=[whole(), whole()],
        out_shape=[shape, shape],
        scratch_shapes=[pltpu.VMEM((tokens, pair), BF16)],
        compiler_params=params(),
        cost_estimate=cost(0, 8 * tokens * pair),
    )(place, *blocks)


def contract(grad_ref, refs, pieces, scale):
    total, row = None, 0
    for ref, (piece, offset, size) in zip(refs, pieces):
        depth = piece.shape[0]
        value = ref[:, offset : offset + size]
        part = jnp.dot(grad_ref[:, row : row + depth], value, preferred_element_type=F32)
        total = part if total is None else total + part
        row += depth
    return total * scale


def their_product(theirs, pieces, scale):
    def body(grad_ref, *refs):
        refs[-1][...] = contract(grad_ref, refs[:-1], pieces, scale).astype(BF16)

    block, tokens = theirs.shape
    size = pieces[0][2]
    return pl.pallas_call(
        body,
        in_specs=[whole()] * (1 + len(pieces)),
        out_specs=whole(),
        out_shape=jax.ShapeDtypeStruct((block, size), BF16),
        compiler_params=params(),
        cost_estimate=cost(2 * block * tokens * size, 4 * tokens * size),
    )(theirs, *[piece for piece, _, _ in pieces])


def write_columns(place, result, mine, products, backs, width, scale):
    block, tokens = mine.shape
    half = width // 2
    flat = [piece for pieces, _ in products for piece, _, _ in pieces]
    sizes = [pieces[0][2] for pieces, _ in products] + [back.shape[1] for back, _ in backs]
    first = 0 if result is None else 1

    def body(place_ref, grad_ref, *refs):
        refs = refs[first:]
        piece_refs, back_refs = refs[: len(flat)], refs[len(flat) : len(flat) + len(backs)]
        out_ref, held_ref, sems = refs[len(flat) + len(backs) :]
        copies = []

        def store(bit, column, size, value):
            slot = len(copies)
            here = held_ref.at[:, pl.ds(sum(sizes[:slot]), size)]
            here[...] = value
            to = pl.ds(pl.multiple_of(bit * half + column, 128), size)
            copies.append(pltpu.make_async_copy(here, out_ref.at[:, to], sems.at[slot]))
            copies[-1].start()

        at = 0
        for pieces, column in products:
            value = contract(grad_ref, piece_refs[at : at + len(pieces)], pieces, scale)
            store(place_ref[0], column, pieces[0][2], value)
            at += len(pieces)
        for ref, (back, column) in zip(back_refs, backs):
            store(1 - place_ref[0], column, back.shape[1], ref[...].astype(F32))
        for copy in copies:
            copy.wait()

    held = [] if result is None else [result]
    return pl.pallas_call(
        body,
        in_specs=[pl.BlockSpec(memory_space=pltpu.SMEM), whole() if products else pl.BlockSpec(memory_space=pl.ANY)]
        + [pl.BlockSpec(memory_space=pl.ANY)] * first
        + [whole()] * (len(flat) + len(backs)),
        out_specs=pl.BlockSpec(memory_space=pl.ANY),
        out_shape=jax.ShapeDtypeStruct((block, width), F32),
        input_output_aliases={2: 0} if first else {},
        scratch_shapes=[pltpu.VMEM((block, sum(sizes)), F32), pltpu.SemaphoreType.DMA((len(sizes),))],
        compiler_params=params(),
        cost_estimate=cost(2 * block * tokens * sum(sizes) if products else 0, 4 * block * sum(sizes)),
    )(place, mine, *held, *flat, *[back for back, _ in backs])


def after(value, *others):
    return lax.optimization_barrier((value, *others))[0]


def plane_plan(pre_act, out_grad, w_up, w_down):
    at, shard = lax.axis_index("dp"), lax.axis_index("tensor")
    z, x = at // 2, at % 2
    y, core = shard // 2, shard % 2
    place = jnp.stack([x, shard]).astype(jnp.int32)
    rows, width = out_grad.shape
    tokens, units = pre_act.shape
    half = units // 2
    pair = width // 4
    scale = 1.0 / math.sqrt(tokens * 8)
    head = half // 3
    tail = half // 4
    middle = half - head - tail

    def columns(pre, bit, offset, size):
        low = pre[:, offset : offset + size]
        high = pre[:, half + offset : half + offset + size]
        return gelu_value_of(either(bit, low, high))

    kept0, sent0 = columns(pre_act, x, 0, head), columns(pre_act, 1 - x, 0, head)
    got0 = xor_permute(sent0, "dp", 1)
    later_act = after(pre_act, sent0)
    kept, sent = columns(later_act, x, head, half - head), columns(later_act, 1 - x, head, half - head)
    got = xor_permute(sent, "dp", 1)
    own0 = jnp.concatenate([kept0, got0])
    far0 = xor_permute(own0, "dp", 4)
    near0 = xor_permute(own0, "dp", 2)

    other = xor_permute(after(out_grad, sent0), "tensor", 2)
    rows_y = jnp.stack([either(y, out_grad, other), either(y, other, out_grad)])
    other = xor_permute(rows_y, "tensor", 1)
    group = jnp.stack([either(core, rows_y, other), either(core, other, rows_y)], axis=1).reshape(tokens, width)

    later_grad = after(out_grad, own0)

    def slab(k):
        return lax.dynamic_slice(later_grad, (0, (z ^ k) * pair), (rows, pair))

    grad = jnp.stack([slab(0)] + [xor_permute(slab(k), "dp", 2 * k) for k in (1, 2, 3)])
    grad_x = xor_permute(grad, "dp", 1)
    both_x = jnp.stack([grad, grad_x])
    grads = [xor_permute(both_x, "tensor", i) for i in (1, 2, 3)]

    own = jnp.concatenate([kept, got])
    joint = xor_permute(after(jnp.concatenate([far0, own[:, :middle]], axis=1), near0), "dp", 2)
    far = xor_permute(after(own, far0, near0), "dp", 4)

    group = after(group, own, grad_x, far0, near0)
    hidden_grad = lax.dot_general(group, w_down, (((1,), (1,)), ((), ())), preferred_element_type=F32)
    pre_grad = (hidden_grad * gelu_slope_of(pre_act)).astype(BF16)
    partial = lax.dot_general(pre_grad, w_up, (((1,), (1,)), ((), ())), preferred_element_type=F32)

    joint, *grads = lax.optimization_barrier((joint, *grads, partial))[:-1]
    mine, theirs = prepare(place, [both_x, *grads])
    pieces0 = [(p, 0, head) for p in (own0, far0, near0, joint)]
    their0 = their_product(theirs, pieces0, scale)
    back0 = xor_permute(their0, "dp", 1)
    far = after(far, their0)
    last = xor_permute(far[:, :middle], "dp", 2)
    pieces1 = [(own, 0, middle), (far, 0, middle), (joint, head, middle), (last, 0, middle)]
    their1 = their_product(theirs, pieces1, scale)
    back1 = xor_permute(their1, "dp", 1)
    ends = xor_permute(jnp.concatenate([own[:, middle:], far[:, middle:]]), "dp", 2)
    pieces2 = [(own, middle, tail), (far, middle, tail), (ends, 0, tail)]
    their2 = their_product(theirs, pieces2, scale)
    back2 = xor_permute(their2, "dp", 1)
    products = [(pieces0, 0), (pieces1, head), (pieces2, head + middle)]
    backs = [(back0, 0), (back1, head), (back2, head + middle)]

    partial = after(partial, their0).reshape(2, 2, rows, width)
    keep = either(core, partial[:, 0], partial[:, 1])
    give = either(core, partial[:, 1], partial[:, 0])
    keep = keep + xor_permute(give, "tensor", 1)
    in_grad = either(y, keep[0], keep[1]) + xor_permute(either(y, keep[1], keep[0]), "tensor", 2)

    result = write_columns(place, None, after(mine, their2), products, backs[:1], units, scale)
    result = write_columns(place, result, mine, [], backs[1:2], units, scale)
    in_grad = in_grad.astype(BF16)
    result = write_columns(place, after(result, in_grad), mine, [], backs[2:], units, scale)
    return (in_grad, result)


def solution(mesh):
    plan = plane_plan if (mesh.shape["dp"], mesh.shape["tensor"]) == (8, 4) else gathered_plan
    placed = (P("dp", "tensor"), P(("dp", "tensor"), None), P(None, "tensor"), P("tensor", None))
    return jax.shard_map(
        plan,
        mesh=mesh,
        in_specs=placed,
        out_specs=(P(("dp", "tensor"), None), P("dp", "tensor")),
        check_vma=False,
    )
```

```python
import math

import jax
import jax.numpy as jnp
from jax import lax
from jax.experimental import pallas as pl
from jax.experimental.pallas import tpu as pltpu
from jax.sharding import PartitionSpec as P

BF16 = jnp.bfloat16
F32 = jnp.float32


def gelu_value_of(pre):
    pre_float = pre.astype(F32)
    normal_cdf = 0.5 * (1.0 + jax.scipy.special.erf(pre_float / math.sqrt(2.0)))
    return (pre_float * normal_cdf).astype(BF16)


def gelu_slope_of(pre):
    pre_float = pre.astype(F32)
    normal_cdf = 0.5 * (1.0 + jax.scipy.special.erf(pre_float / math.sqrt(2.0)))
    density = jnp.exp(-0.5 * pre_float * pre_float) / math.sqrt(2.0 * math.pi)
    return normal_cdf + pre_float * density


def xor_permute(value, axis, mask):
    count = lax.axis_size(axis)
    return lax.ppermute(value, axis, [(i, i ^ mask) for i in range(count)])


def either(bit, low, high):
    return jnp.where(bit == 0, low, high)


def gathered_plan(pre_act, out_grad, w_up, w_down):
    act = gelu_value_of(pre_act)
    gathered = lax.all_gather(out_grad, "tensor", axis=0, tiled=True)
    hidden_grad = lax.dot_general(gathered, w_down, (((1,), (1,)), ((), ())), preferred_element_type=F32)
    pre_grad = (hidden_grad * gelu_slope_of(pre_act)).astype(BF16)
    all_tokens = gathered.shape[0] * lax.axis_size("dp")
    my_columns = lax.all_to_all(gathered, "dp", split_axis=1, concat_axis=0, tiled=True)
    summed = lax.dot_general(
        my_columns,
        lax.all_gather(act, "dp", axis=0, tiled=True),
        (((0,), (0,)), ((), ())),
        preferred_element_type=F32,
    )
    in_grad = lax.psum_scatter(
        lax.dot_general(pre_grad, w_up, (((1,), (1,)), ((), ())), preferred_element_type=F32),
        "tensor",
        scatter_dimension=0,
        tiled=True,
    ).astype(BF16)
    return (in_grad, summed / math.sqrt(all_tokens))


VMEM_LIMIT = 16 * 1024 * 1024


def params():
    return pltpu.CompilerParams(vmem_limit_bytes=VMEM_LIMIT)


def cost(flops, moved):
    return pl.CostEstimate(flops=flops, bytes_accessed=moved, transcendentals=0)


def whole():
    return pl.BlockSpec(memory_space=pltpu.VMEM)


def prepare(place, blocks):
    _, depth, rows, pair = blocks[0].shape
    block = pair // 2
    tokens = 2 * depth * len(blocks) * rows

    def body(place_ref, *refs):
        mine_ref, theirs_ref, held_ref = refs[len(blocks) :]
        x, shard = place_ref[0], place_ref[1]
        for i, ref in enumerate(refs[: len(blocks)]):
            for k in range(depth):
                for j in range(2):
                    at = ((2 * (k % 2 * 2 + k // 2) + j) * len(blocks) + (i ^ shard)) * rows
                    held_ref[pl.ds(pl.multiple_of(at, rows), rows), :] = ref[j, k]
        for out, bit in ((mine_ref, x), (theirs_ref, 1 - x)):
            columns = pl.ds(pl.multiple_of(bit * block, 128), block)
            out[...] = held_ref[:, columns].T

    shape = jax.ShapeDtypeStruct((block, tokens), BF16)
    return pl.pallas_call(
        body,
        in_specs=[pl.BlockSpec(memory_space=pltpu.SMEM)] + [whole()] * len(blocks),
        out_specs=[whole(), whole()],
        out_shape=[shape, shape],
        scratch_shapes=[pltpu.VMEM((tokens, pair), BF16)],
        compiler_params=params(),
        cost_estimate=cost(0, 8 * tokens * pair),
    )(place, *blocks)


def contract(grad_ref, refs, pieces, scale):
    total, row = None, 0
    for ref, (piece, offset, size) in zip(refs, pieces):
        depth = piece.shape[0]
        value = ref[:, offset : offset + size]
        part = jnp.dot(grad_ref[:, row : row + depth], value, preferred_element_type=F32)
        total = part if total is None else total + part
        row += depth
    return total * scale


def their_product(theirs, pieces, scale):
    def body(grad_ref, *refs):
        refs[-1][...] = contract(grad_ref, refs[:-1], pieces, scale).astype(BF16)

    block, tokens = theirs.shape
    size = pieces[0][2]
    return pl.pallas_call(
        body,
        in_specs=[whole()] * (1 + len(pieces)),
        out_specs=whole(),
        out_shape=jax.ShapeDtypeStruct((block, size), BF16),
        compiler_params=params(),
        cost_estimate=cost(2 * block * tokens * size, 4 * tokens * size),
    )(theirs, *[piece for piece, _, _ in pieces])


def write_columns(place, result, mine, products, backs, width, scale):
    block, tokens = mine.shape
    half = width // 2
    flat = [piece for pieces, _ in products for piece, _, _ in pieces]
    sizes = [pieces[0][2] for pieces, _ in products] + [back.shape[1] for back, _ in backs]
    first = 0 if result is None else 1

    def body(place_ref, grad_ref, *refs):
        refs = refs[first:]
        piece_refs, back_refs = refs[: len(flat)], refs[len(flat) : len(flat) + len(backs)]
        out_ref, held_ref, sems = refs[len(flat) + len(backs) :]
        copies = []

        def store(bit, column, size, value):
            slot = len(copies)
            here = held_ref.at[:, pl.ds(sum(sizes[:slot]), size)]
            here[...] = value
            to = pl.ds(pl.multiple_of(bit * half + column, 128), size)
            copies.append(pltpu.make_async_copy(here, out_ref.at[:, to], sems.at[slot]))
            copies[-1].start()

        at = 0
        for pieces, column in products:
            value = contract(grad_ref, piece_refs[at : at + len(pieces)], pieces, scale)
            store(place_ref[0], column, pieces[0][2], value)
            at += len(pieces)
        for ref, (back, column) in zip(back_refs, backs):
            store(1 - place_ref[0], column, back.shape[1], ref[...].astype(F32))
        for copy in copies:
            copy.wait()

    held = [] if result is None else [result]
    return pl.pallas_call(
        body,
        in_specs=[pl.BlockSpec(memory_space=pltpu.SMEM), whole() if products else pl.BlockSpec(memory_space=pl.ANY)]
        + [pl.BlockSpec(memory_space=pl.ANY)] * first
        + [whole()] * (len(flat) + len(backs)),
        out_specs=pl.BlockSpec(memory_space=pl.ANY),
        out_shape=jax.ShapeDtypeStruct((block, width), F32),
        input_output_aliases={2: 0} if first else {},
        scratch_shapes=[pltpu.VMEM((block, sum(sizes)), F32), pltpu.SemaphoreType.DMA((len(sizes),))],
        compiler_params=params(),
        cost_estimate=cost(2 * block * tokens * sum(sizes) if products else 0, 4 * block * sum(sizes)),
    )(place, mine, *held, *flat, *[back for back, _ in backs])


def after(value, *others):
    return lax.optimization_barrier((value, *others))[0]


def plane_plan(pre_act, out_grad, w_up, w_down):
    at, shard = lax.axis_index("dp"), lax.axis_index("tensor")
    z, x = at // 2, at % 2
    y, core = shard // 2, shard % 2
    place = jnp.stack([x, shard]).astype(jnp.int32)
    rows, width = out_grad.shape
    tokens, units = pre_act.shape
    half = units // 2
    pair = width // 4
    scale = 1.0 / math.sqrt(tokens * 8)
    head = half // 4
    tail = half // 3
    middle = half - head - tail

    def columns(pre, bit, offset, size):
        low = pre[:, offset : offset + size]
        high = pre[:, half + offset : half + offset + size]
        return gelu_value_of(either(bit, low, high))

    kept0, sent0 = columns(pre_act, x, 0, head), columns(pre_act, 1 - x, 0, head)
    got0 = xor_permute(sent0, "dp", 1)
    later_act = after(pre_act, sent0)
    kept, sent = columns(later_act, x, head, half - head), columns(later_act, 1 - x, head, half - head)
    got = xor_permute(sent, "dp", 1)
    own0 = jnp.concatenate([kept0, got0])
    far0 = xor_permute(own0, "dp", 4)
    near0 = xor_permute(own0, "dp", 2)

    other = xor_permute(after(out_grad, sent0), "tensor", 2)
    rows_y = jnp.stack([either(y, out_grad, other), either(y, other, out_grad)])
    other = xor_permute(rows_y, "tensor", 1)
    group = jnp.stack([either(core, rows_y, other), either(core, other, rows_y)], axis=1).reshape(tokens, width)

    later_grad = after(out_grad, own0)

    def slab(k):
        return lax.dynamic_slice(later_grad, (0, (z ^ k) * pair), (rows, pair))

    grad = jnp.stack([slab(0)] + [xor_permute(slab(k), "dp", 2 * k) for k in (1, 2, 3)])
    grad_x = xor_permute(grad, "dp", 1)
    both_x = jnp.stack([grad, grad_x])
    grads = [xor_permute(both_x, "tensor", i) for i in (1, 2, 3)]

    own = jnp.concatenate([kept, got])
    joint = xor_permute(after(jnp.concatenate([far0, own[:, :middle]], axis=1), near0), "dp", 2)
    far = xor_permute(after(own, far0, near0), "dp", 4)

    group = after(group, own, grad_x, far0, near0)
    hidden_grad = lax.dot_general(group, w_down, (((1,), (1,)), ((), ())), preferred_element_type=F32)
    pre_grad = (hidden_grad * gelu_slope_of(pre_act)).astype(BF16)
    partial = lax.dot_general(pre_grad, w_up, (((1,), (1,)), ((), ())), preferred_element_type=F32)

    joint, *grads = lax.optimization_barrier((joint, *grads, partial))[:-1]
    mine, theirs = prepare(place, [both_x, *grads])
    pieces0 = [(p, 0, head) for p in (own0, far0, near0, joint)]
    their0 = their_product(theirs, pieces0, scale)
    back0 = xor_permute(their0, "dp", 1)
    far = after(far, their0)
    last = xor_permute(far[:, :middle], "dp", 2)
    pieces1 = [(own, 0, middle), (far, 0, middle), (joint, head, middle), (last, 0, middle)]
    their1 = their_product(theirs, pieces1, scale)
    back1 = xor_permute(their1, "dp", 1)
    ends = xor_permute(jnp.concatenate([own[:, middle:], far[:, middle:]]), "dp", 2)
    pieces2 = [(own, middle, tail), (far, middle, tail), (ends, 0, tail)]
    their2 = their_product(theirs, pieces2, scale)
    back2 = xor_permute(their2, "dp", 1)
    products = [(pieces0, 0), (pieces1, head), (pieces2, head + middle)]
    backs = [(back0, 0), (back1, head), (back2, head + middle)]

    partial = after(partial, their0).reshape(2, 2, rows, width)
    keep = either(core, partial[:, 0], partial[:, 1])
    give = either(core, partial[:, 1], partial[:, 0])
    keep = keep + xor_permute(give, "tensor", 1)
    in_grad = either(y, keep[0], keep[1]) + xor_permute(either(y, keep[1], keep[0]), "tensor", 2)

    result = write_columns(place, None, after(mine, their2), products, backs[:1], units, scale)
    result = write_columns(place, result, mine, [], backs[1:2], units, scale)
    in_grad = in_grad.astype(BF16)
    result = write_columns(place, after(result, in_grad), mine, [], backs[2:], units, scale)
    return (in_grad, result)


def solution(mesh):
    plan = plane_plan if (mesh.shape["dp"], mesh.shape["tensor"]) == (8, 4) else gathered_plan
    placed = (P("dp", "tensor"), P(("dp", "tensor"), None), P(None, "tensor"), P("tensor", None))
    return jax.shard_map(
        plan,
        mesh=mesh,
        in_specs=placed,
        out_specs=(P(("dp", "tensor"), None), P("dp", "tensor")),
        check_vma=False,
    )
```
